256 devices in a mesh: seq: 64 (over x, z, y_lo), head: 4 (over y_hi, core).
Axes of the slice: x: 4, y: 4 (y_hi: 2, y_lo: 2; y = y_hi * 2 + y_lo), z: 8, core: 2. Of those that a mesh axis runs over, the one named last changes fastest.
Arguments:
- queries: bfloat16 [8192, 1536], P('seq', 'head'), may hold values from -8 to 8
- cell_types: int32 [8192], P('seq'), may hold values from 0 to 127
- promoters: int32 [8192], P('seq'), may hold values from 0 to 131071, as said below
- offsets: int32 [8192], P('seq'), may hold values from -64 to 64, as said below
- cell_embed: bfloat16 [128, 1536], P(None, 'head'), may hold values from -3 to 3
- bin_keys: bfloat16 [131072, 1536], P('seq', 'head'), may hold values from -6 to 6
- bin_values: bfloat16 [131072, 1536], P('seq', 'head'), may hold values from -6 to 6
- slopes: float32 [16], P('head'), may hold values from 1.280082e-05 to 0.05
- w_out: bfloat16 [1536, 1536], P('head'), may hold values from -0.15625 to 0.15625
Outputs:
- pooled_features: bfloat16 [8192, 1536], P('seq', 'head')
The draws below stay inside these ranges and needn't reach their ends.
Inputs may be any that keep to these rules, and one draw needn't show every extreme that they name: `promoters`: the promoter of row r lies in bins (r // 128) * 2048 to (r // 128 + 1) * 2048 - 1; in each aligned block of 128 rows, the block's first row sits at the first of those bins and its second row at the last. `offsets`: in each aligned block of 128 rows the first row has offset -64 and the second row 64.
All inputs are finite; a program needn't handle non-finite values.
Results may differ from the reference program's by a relative error of at most 0.012.
Values may be sent and summed in bfloat16 or wider, within the bound.
No kernel may reach another device: no remote copies, remote signals or barrier semaphores. Data moves between devices by JAX's collectives and lax.ppermute only.
A program may use at most 128 MiB of HBM per device.

```python
import math
import jax
import jax.numpy as jnp
from jax import lax

HEADS = 16
HEAD_DIM = 96
D = 1536
CT = 128
BIN_DEV = 2048
Q_DEV = 128
RADIUS = 7812
SHIFT = 64
HOPS = 4
BINS = 131072
Q_ALL = 8192
N_SEQ = 64


def positions(key):
    base = jax.random.fold_in(key, 7101)
    first, second, third = jax.random.split(base, 3)
    index = jnp.arange(Q_ALL, dtype=jnp.int32)
    block = index // Q_DEV
    within = index % Q_DEV
    inner = jnp.minimum(jax.random.randint(first, (Q_ALL,), 0, BIN_DEV), jax.random.randint(second, (Q_ALL,), 0, BIN_DEV))
    inner = jnp.where(within == 0, 0, jnp.where(within == 1, BIN_DEV - 1, inner))
    shifts = jax.random.randint(third, (Q_ALL,), -SHIFT, SHIFT + 1)
    shifts = jnp.where(within == 0, -SHIFT, jnp.where(within == 1, SHIFT, shifts))
    return ((block * BIN_DEV + inner).astype(jnp.int32), shifts.astype(jnp.int32))


def draw_promoters(key, part):
    return positions(key)[0]


def draw_offsets(key, part):
    return positions(key)[1]


def draw_bin_keys(key, part):
    inner_key = jax.random.fold_in(key, 7202)
    table = jnp.clip(jax.random.normal(inner_key, (BINS, D)), -6.0, 6.0)
    return table.astype(jnp.bfloat16)


def draw_queries(key, part):
    inner_key = jax.random.fold_in(key, 7303)
    table = jnp.clip(jax.random.normal(inner_key, (Q_ALL, D)), -6.0, 6.0)
    return table.astype(jnp.bfloat16)


def set_ends(entries, rng, least, largest):
    place = [jax.random.randint(jax.random.fold_in(rng, axis), (), 0, length) for axis, length in enumerate(entries.shape)]
    main_axis = entries.shape.index(max(entries.shape))
    neighbour = place[:main_axis] + [(place[main_axis] + 1) % entries.shape[main_axis]] + place[main_axis + 1:]
    return entries.at[tuple(place)].set(least).at[tuple(neighbour)].set(largest)


def block_scale(stream_key, dims, pieces, least, largest):
    level, own = 1.0, jax.random.fold_in(stream_key, 6)
    for dim, shards_of in pieces:
        steps = jnp.exp(jax.random.uniform(jax.random.fold_in(own, dim), (shards_of,), jnp.float32, least / len(pieces), largest / len(pieces)))
        level = level * jnp.repeat(steps, dims[dim] // shards_of).reshape([-1 if axis == dim else 1 for axis in range(len(dims))])
    return level


def noise(stream_key, extent, spread, reach, cuts=(), kind=jnp.bfloat16):
    loudness = block_scale(stream_key, extent, cuts, -0.22, 0.18) if cuts else 1.0
    entries = jax.random.normal(stream_key, extent, jnp.float32) * spread * loudness
    return jnp.minimum(jnp.maximum(entries, -reach), reach).astype(kind)


def setup_inputs(seed: int = 0) -> dict:
    seeds = jax.random.split(jax.random.key(seed), 10)
    queries = draw_queries(jax.random.fold_in(seeds[9], 71), 0)
    cell_types = set_ends(jax.random.randint(seeds[1], (Q_ALL,), 0, CT), jax.random.fold_in(seeds[1], 1), 0, CT - 1).astype(jnp.int32)
    promoters = draw_promoters(jax.random.fold_in(seeds[9], 71), 0)
    offsets = draw_offsets(jax.random.fold_in(seeds[9], 71), 0)
    cell_embed = noise(seeds[4], (CT, D), 0.5, 3.0, ((1, 4),))
    bin_keys = draw_bin_keys(jax.random.fold_in(seeds[9], 71), 0)
    bin_values = noise(seeds[6], (BINS, D), 1.0, 6.0, ((0, 64), (1, 4)))
    slopes = jnp.clip(jnp.exp(math.log(0.05) - 8.270269 * jax.random.uniform(seeds[7], (HEADS,), jnp.float32) ** block_scale(seeds[7], (HEADS,), ((0, 4),), -0.2, 0.2)), 1.2800819604308344e-05, 0.05)
    w_out = noise(seeds[8], (D, D), D ** -0.5, 0.15625, ((0, 4),))
    return dict(queries=queries, cell_types=cell_types, promoters=promoters, offsets=offsets, cell_embed=cell_embed, bin_keys=bin_keys, bin_values=bin_values, slopes=slopes, w_out=w_out)


def reference(queries, cell_types, promoters, offsets, cell_embed, bin_keys, bin_values, slopes, w_out):
    embedded = cell_embed.astype(jnp.float32)[cell_types]
    query_rows = (queries.astype(jnp.float32) + embedded).astype(jnp.bfloat16)
    centres = promoters + offsets
    padding = HOPS * BIN_DEV
    keys_padded = jnp.pad(bin_keys, ((padding, padding), (0, 0)))
    values_padded = jnp.pad(bin_values, ((padding, padding), (0, 0)))
    window_len = (2 * HOPS + 1) * BIN_DEV
    scale = HEAD_DIM ** -0.5

    def one_shard(shard):
        shard_rows = lax.dynamic_slice_in_dim(query_rows, shard * Q_DEV, Q_DEV, 0)
        shard_centres = lax.dynamic_slice_in_dim(centres, shard * Q_DEV, Q_DEV, 0)
        shard_keys = lax.dynamic_slice_in_dim(keys_padded, shard * BIN_DEV, window_len, 0)
        shard_values = lax.dynamic_slice_in_dim(values_padded, shard * BIN_DEV, window_len, 0)
        bin_index = (shard - HOPS) * BIN_DEV + jnp.arange(window_len, dtype=jnp.int32)
        distance = jnp.abs(bin_index[None, :] - shard_centres[:, None])
        usable = (distance <= RADIUS) & (bin_index[None, :] >= 0) & (bin_index[None, :] < BINS)
        distance_float = distance.astype(jnp.float32)
        head_queries = shard_rows.reshape(Q_DEV, HEADS, HEAD_DIM).transpose(1, 0, 2)
        head_keys = shard_keys.reshape(window_len, HEADS, HEAD_DIM).transpose(1, 0, 2)
        head_values = shard_values.reshape(window_len, HEADS, HEAD_DIM).transpose(1, 0, 2)

        def one_head(inputs):
            query_head, key_head, value_head, slope = inputs
            scores = jnp.dot(query_head, key_head.T, preferred_element_type=jnp.float32) * scale
            scores = scores - slope * distance_float
            scores = jnp.where(usable, scores, -1e30)
            row_max = jnp.max(scores, axis=1, keepdims=True)
            exps = jnp.where(usable, jnp.exp(scores - row_max), 0.0)
            totals = jnp.sum(exps, axis=1)
            weights = exps.astype(jnp.bfloat16)
            pooled_head = jnp.dot(weights, value_head, preferred_element_type=jnp.float32)
            return pooled_head / totals[:, None]

        pooled_heads = lax.map(one_head, (head_queries, head_keys, head_values, slopes))
        return pooled_heads.transpose(1, 0, 2).reshape(Q_DEV, D).astype(jnp.bfloat16)

    pooled = lax.map(one_shard, jnp.arange(N_SEQ, dtype=jnp.int32)).reshape(Q_ALL, D)
    return jnp.dot(pooled, w_out, preferred_element_type=jnp.float32).astype(jnp.bfloat16)
```

```python
import functools
import math

import jax
import jax.numpy as jnp
from jax import lax
from jax.experimental import pallas as pl
from jax.experimental.pallas import tpu as pltpu
from jax.sharding import PartitionSpec as P

HEAD_DIM = 96
RADIUS = 7812
SHIFT = 64
HOPS = 4
LANES = 128
LOG2E = math.log2(math.e)
SCALE2 = LOG2E / math.sqrt(HEAD_DIM)
EMPTY = -16384.0
SUM_LO, SUM_HI = 2.0**-60, 2.0**100
TILE = 512


def column(row):
    n = row.shape[1]
    eye = lax.broadcasted_iota(jnp.int32, (n, n), 0) == lax.broadcasted_iota(jnp.int32, (n, n), 1)
    return jnp.sum(jnp.where(eye, row, 0.0), axis=1, keepdims=True)


def query_kernel(groups, types_ref, promoters_ref, offsets_ref, base_ref, queries_ref, embed_ref, out_ref):
    rows = queries_ref.shape[0]
    kinds = embed_ref.shape[0]
    one_hot = (lax.broadcasted_iota(jnp.int32, (kinds, rows), 0) == types_ref[...]).astype(jnp.float32)
    embedded = lax.dot_general(
        one_hot.T.astype(jnp.bfloat16), embed_ref[...], (((1,), (0,)), ((), ())), preferred_element_type=jnp.float32
    )
    query = (queries_ref[...].astype(jnp.float32) + embedded).astype(jnp.bfloat16)
    place = promoters_ref[...] + offsets_ref[...] - base_ref[0] + SHIFT
    coarse = lax.shift_right_arithmetic(place, 4)
    fine = place - coarse * 16
    coarse = column((coarse * 16).astype(jnp.float32))
    fine = column(fine.astype(jnp.float32))
    lane = lax.broadcasted_iota(jnp.int32, (rows, LANES - HEAD_DIM), 1)
    extra = jnp.where(lane == 0, coarse, jnp.where(lane == 1, fine, 0.0)).astype(jnp.bfloat16)
    for g in range(groups):
        out_ref[:, g * LANES : g * LANES + HEAD_DIM] = query[:, g * HEAD_DIM : (g + 1) * HEAD_DIM]
        out_ref[:, g * LANES + HEAD_DIM : (g + 1) * LANES] = extra


def bins_kernel(groups, keys_ref, values_ref, keys_out, values_out):
    count = keys_ref.shape[0]
    lane = lax.broadcasted_iota(jnp.int32, (count, LANES - HEAD_DIM), 1)
    blank = jnp.zeros((count, LANES - HEAD_DIM), jnp.bfloat16)
    ones = jnp.where(lane == 0, 1.0, 0.0).astype(jnp.bfloat16)
    for g in range(groups):
        keys_out[g, :, :HEAD_DIM] = keys_ref[:, g * HEAD_DIM : (g + 1) * HEAD_DIM]
        keys_out[g, :, HEAD_DIM:] = blank
        values_out[g, :, :HEAD_DIM] = values_ref[:, g * HEAD_DIM : (g + 1) * HEAD_DIM]
        values_out[g, :, HEAD_DIM:] = ones


def unit_kernel(strides, bins, slopes_ref, ok_ref, *refs):
    n = len(strides)
    query_refs, (keys_ref, values_ref), out_refs, (acc_ref, bad_ref) = refs[:n], refs[n : n + 2], refs[n + 2 : 2 * n + 2], refs[2 * n + 2 :]
    g = pl.program_id(0)
    rows = query_refs[0].shape[0]
    slope = slopes_ref[g] * LOG2E

    def centre_of(i):
        extra = query_refs[i][:, HEAD_DIM:LANES].astype(jnp.float32)
        place = extra[:, 0:1] + extra[:, 1:2] - SHIFT
        return place - float(bins * strides[i]), None

    @pl.when(g == 0)
    def _():
        for i in range(n):
            extra = query_refs[i][:, HEAD_DIM:LANES].astype(jnp.float32)
            place = extra[:, 0:1] + extra[:, 1:2] - float(SHIFT + bins * strides[i])
            bad_ref[i] = jnp.broadcast_to(place, (rows, LANES))

    def prepared(i):
        centre = bad_ref[i][:, 0:1]
        nearest = jnp.maximum(0.0, jnp.maximum(-centre, centre - float(bins - 1)))
        alive = (nearest <= RADIUS) & (ok_ref[i] > 0)
        return centre, nearest, alive

    def arguments(i, centre, nearest, start, size):
        stride = strides[i]
        query = query_refs[i][:, pl.ds(pl.multiple_of(g * LANES, LANES), LANES)]
        keys = keys_ref[0, pl.ds(start, size), :]
        raw = lax.dot_general(query, keys, (((1,), (1,)), ((), ())), preferred_element_type=jnp.float32)
        position = (start + lax.broadcasted_iota(jnp.int32, (1, size), 1)).astype(jnp.float32)
        if stride >= 2:
            bias = -slope * position
        elif stride <= -2:
            bias = -slope * (float(bins - 1) - position)
        else:
            bias = -slope * (jnp.abs(position - centre) - nearest)
        usable = None
        if stride >= 3:
            usable = position <= centre + float(RADIUS)
        elif stride <= -3:
            usable = position >= centre - float(RADIUS)
        return raw * SCALE2 + bias, usable

    def finish(i, acc, shift, nearest, alive):
        lane = lax.broadcasted_iota(jnp.int32, (rows, LANES), 1)
        exponent = shift - slope * nearest
        coarse = jnp.where(alive, jnp.round(exponent * 0.0625) * 16.0, EMPTY)
        factor = jnp.where(alive, jnp.exp2(exponent - coarse), 0.0)
        scaled = jnp.where(alive, acc * factor, 0.0)
        total = scaled[:, HEAD_DIM : HEAD_DIM + 1]
        high = total.astype(jnp.bfloat16).astype(jnp.float32)
        scaled = jnp.where(lane == HEAD_DIM + 1, total - high, scaled)
        scaled = jnp.where(lane == HEAD_DIM + 2, coarse, scaled)
        return scaled.astype(jnp.bfloat16)

    wrong = jnp.zeros((rows, 1), jnp.float32)
    for i in range(n):
        centre, nearest, alive = prepared(i)
        acc = jnp.zeros((rows, LANES), jnp.float32)
        for start in range(0, bins, TILE):
            logs, usable = arguments(i, centre, nearest, start, TILE)
            weights = jnp.exp2(logs)
            if usable is not None:
                weights = jnp.where(usable, weights, 0.0)
            acc += jnp.dot(weights.astype(jnp.bfloat16), values_ref[0, start : start + TILE, :], preferred_element_type=jnp.float32)
        total = acc[:, HEAD_DIM : HEAD_DIM + 1]
        fine = (total >= SUM_LO) & (total <= SUM_HI)
        wrong = jnp.maximum(wrong, jnp.where(alive & jnp.logical_not(fine), 1.0, 0.0))
        out_refs[i][...] = finish(i, acc, jnp.zeros((rows, 1), jnp.float32), nearest, alive)

    @pl.when(jnp.max(wrong) > 0.0)
    def _():
        for i in range(n):
            centre, nearest, alive = prepared(i)

            def largest(k, so_far):
                logs, usable = arguments(i, centre, nearest, pl.multiple_of(k * LANES, LANES), LANES)
                if usable is not None:
                    logs = jnp.where(usable, logs, -1e30)
                return jnp.maximum(so_far, jnp.max(logs, axis=1, keepdims=True))

            shift = lax.fori_loop(0, bins // LANES, largest, jnp.full((rows, 1), -1e30, jnp.float32))
            acc_ref[...] = jnp.zeros_like(acc_ref)

            @pl.loop(0, bins // LANES)
            def _(k):
                start = pl.multiple_of(k * LANES, LANES)
                logs, usable = arguments(i, centre, nearest, start, LANES)
                weights = jnp.exp2(logs - shift)
                if usable is not None:
                    weights = jnp.where(usable, weights, 0.0)
                acc_ref[...] += jnp.dot(
                    weights.astype(jnp.bfloat16), values_ref[0, pl.ds(start, LANES), :], preferred_element_type=jnp.float32
                )

            out_refs[i][...] = finish(i, acc_ref[...], shift, nearest, alive)


def merge_kernel(groups, place_ref, *refs):
    part_refs, (w_ref, keep_ref, send_ref) = refs[:-3], refs[-3:]
    rows = part_refs[0].shape[0]
    pooled = []
    for g in range(groups):
        parts = [ref[:, g * LANES : (g + 1) * LANES].astype(jnp.float32) for ref in part_refs]
        scales = [part[:, HEAD_DIM + 2 : HEAD_DIM + 3] for part in parts]
        top = functools.reduce(jnp.maximum, scales)
        acc = sum(part * jnp.exp2(scale - top) for part, scale in zip(parts, scales))
        total = acc[:, HEAD_DIM : HEAD_DIM + 1] + acc[:, HEAD_DIM + 1 : HEAD_DIM + 2]
        pooled.append((acc[:, :HEAD_DIM] / total).astype(jnp.bfloat16))
    width = w_ref.shape[1] // 4
    core, high = place_ref[0] & 1, place_ref[0] >> 1
    for k in range(2):
        row = jnp.where(k == 0, high, 1 - high) * 2
        for ref, lane in ((send_ref, 1 - core), (keep_ref, core)):
            start = pl.multiple_of((row + lane) * width, LANES)
            acc = jnp.zeros((rows, width), jnp.float32)
            for g in range(groups):
                weights = w_ref[g * HEAD_DIM : (g + 1) * HEAD_DIM, pl.ds(start, width)]
                acc += jnp.dot(pooled[g], weights, preferred_element_type=jnp.float32)
            ref[k] = acc.astype(ref.dtype)


SMEM = pl.BlockSpec(memory_space=pltpu.SMEM)


def attend(strides, slopes, ok, queries, keys, values):
    groups, bins, _ = keys.shape
    rows, width = queries[0].shape
    n = len(strides)
    return pl.pallas_call(
        functools.partial(unit_kernel, strides, bins),
        grid=(groups,),
        in_specs=[SMEM, SMEM]
        + [pl.BlockSpec((rows, width), lambda g: (0, 0))] * n
        + [pl.BlockSpec((1, bins, LANES), lambda g: (g, 0, 0))] * 2,
        out_specs=[pl.BlockSpec((rows, LANES), lambda g: (0, g))] * n,
        out_shape=[jax.ShapeDtypeStruct((rows, width), jnp.bfloat16)] * n,
        scratch_shapes=[pltpu.VMEM((rows, LANES), jnp.float32), pltpu.VMEM((n, rows, LANES), jnp.float32)],
        compiler_params=pltpu.CompilerParams(vmem_limit_bytes=28 * 2**20),
        cost_estimate=pl.CostEstimate(
            flops=4 * n * rows * bins * width, bytes_accessed=4 * bins * width, transcendentals=n * rows * bins * groups
        ),
        name="attend",
    )(slopes, ok, *queries, keys, values)


def prepare_queries(queries, cell_types, promoters, offsets, cell_embed, base, groups):
    rows = queries.shape[0]
    return pl.pallas_call(
        functools.partial(query_kernel, groups),
        in_specs=[pl.BlockSpec()] * 3 + [SMEM] + [pl.BlockSpec()] * 2,
        out_shape=jax.ShapeDtypeStruct((rows, groups * LANES), jnp.bfloat16),
        compiler_params=pltpu.CompilerParams(vmem_limit_bytes=8 * 2**20),
        name="prepare_queries",
    )(cell_types[None, :], promoters[None, :], offsets[None, :], base[None], queries, cell_embed)


def prepare_bins(keys, values, groups):
    bins = keys.shape[0]
    step = 512
    flat = pl.BlockSpec((step, keys.shape[1]), lambda i: (i, 0))
    split = pl.BlockSpec((groups, step, LANES), lambda i: (0, i, 0))
    return pl.pallas_call(
        functools.partial(bins_kernel, groups),
        grid=(bins // step,),
        in_specs=[flat, flat],
        out_specs=[split, split],
        out_shape=[jax.ShapeDtypeStruct((groups, bins, LANES), jnp.bfloat16)] * 2,
        compiler_params=pltpu.CompilerParams(vmem_limit_bytes=16 * 2**20),
        cost_estimate=pl.CostEstimate(flops=0, bytes_accessed=14 * 2**20, transcendentals=0),
        name="prepare_bins",
    )(keys, values)


def merge(place, parts, w_out, groups):
    rows = parts[0].shape[0]
    width = w_out.shape[1] // 4
    return pl.pallas_call(
        functools.partial(merge_kernel, groups),
        in_specs=[SMEM] + [pl.BlockSpec()] * (len(parts) + 1),
        out_shape=[
            jax.ShapeDtypeStruct((2, rows, width), jnp.float32),
            jax.ShapeDtypeStruct((2, rows, width), jnp.bfloat16),
        ],
        compiler_params=pltpu.CompilerParams(vmem_limit_bytes=16 * 2**20),
        name="merge",
    )(place[None], *parts, w_out)


def pairings(stride, count):
    ring = math.gcd(stride, count)
    length = count // ring
    even, odd = [], []
    for first in range(ring):
        order = [(first + stride * k) % count for k in range(length)]
        for k in range(0, length, 2):
            for table, a, b in ((even, order[k], order[k + 1]), (odd, order[k + 1], order[(k + 2) % length])):
                table += [(a, b), (b, a)]
    return even, odd


def rotated(value, steps):
    count = lax.axis_size("seq")
    return lax.ppermute(value, "seq", [(i, (i + steps) % count) for i in range(count)])


def local(queries, cell_types, promoters, offsets, cell_embed, bin_keys, bin_values, slopes, w_out):
    seq_count = lax.axis_size("seq")
    position = lax.axis_index("seq")
    place = lax.axis_index("head")
    bins = bin_keys.shape[0]
    groups = slopes.shape[0]
    mine = prepare_queries(queries, cell_types, promoters, offsets, cell_embed, position * bins, groups)
    strides = [1, 2, 3, 4]
    arrived = [(rotated(mine, d), rotated(mine, -d)) for d in strides]
    keys, values = prepare_bins(bin_keys, bin_values, groups)
    parts = list(attend((0,), slopes, jnp.ones((1,), jnp.int32), (mine,), keys, values))
    for d, pair in zip(strides, arrived):
        ok = jnp.stack([position >= d, position < seq_count - d]).astype(jnp.int32)
        up, down = attend((d, -d), slopes, ok, pair, keys, values)
        parts += [rotated(up, -d), rotated(down, d)]
    keep, send = merge(place, parts, w_out, groups)
    got = lax.ppermute(send, "head", [(i, i ^ 1) for i in range(4)])
    other = (keep[1] + got[1].astype(jnp.float32)).astype(jnp.bfloat16)
    last = lax.ppermute(other, "head", [(i, i ^ 2) for i in range(4)])
    return (keep[0] + got[0].astype(jnp.float32) + last.astype(jnp.float32)).astype(jnp.bfloat16)


def solution(mesh):
    return jax.shard_map(
        local,
        mesh=mesh,
        in_specs=(
            P("seq", "head"),
            P("seq"),
            P("seq"),
            P("seq"),
            P(None, "head"),
            P("seq", "head"),
            P("seq", "head"),
            P("head"),
            P("head", None),
        ),
        out_specs=P("seq", "head"),
        check_vma=False,
    )
```

```python
import functools
import math

import jax
import jax.numpy as jnp
from jax import lax
from jax.experimental import pallas as pl
from jax.experimental.pallas import tpu as pltpu
from jax.sharding import PartitionSpec as P

HEAD_DIM = 96
RADIUS = 7812
SHIFT = 64
LANES = 128
LOG2E = math.log2(math.e)
SCALE2 = LOG2E / math.sqrt(HEAD_DIM)
FAR = 1e30
EMPTY = -16384.0
SUM_LO, SUM_HI = 2.0**-60, 2.0**100
TILE = 512
QUERY_VMEM = 4 * 2**20
BINS_VMEM = 16 * 2**20
OVER_ROWS = (((1,), (1,)), ((), ()))

SMEM = pl.BlockSpec(memory_space=pltpu.SMEM)
VMEM = pl.BlockSpec(memory_space=pltpu.VMEM)
HBM = pl.BlockSpec(memory_space=pltpu.HBM)


def column(row):
    n = row.shape[1]
    eye = lax.broadcasted_iota(jnp.int32, (n, n), 0) == lax.broadcasted_iota(jnp.int32, (n, n), 1)
    return jnp.sum(jnp.where(eye, row, 0.0), axis=1, keepdims=True)


def query_kernel(groups, base_ref, *refs):
    sources, out_ref, copies, sems = refs[:5], refs[5], refs[6:11], refs[11]
    moves = [pltpu.make_async_copy(a, b, sems.at[i]) for i, (a, b) in enumerate(zip(sources, copies))]
    for move in moves:
        move.start()
    for move in moves:
        move.wait()
    types_ref, promoters_ref, offsets_ref, queries_ref, embed_ref = copies
    rows = queries_ref.shape[0]
    kinds = embed_ref.shape[0]
    one_hot = (lax.broadcasted_iota(jnp.int32, (kinds, rows), 0) == types_ref[...]).astype(jnp.float32)
    embedded = jnp.dot(one_hot.T.astype(jnp.bfloat16), embed_ref[...], preferred_element_type=jnp.float32)
    query = (queries_ref[...].astype(jnp.float32) + embedded).astype(jnp.bfloat16)
    place = promoters_ref[...] + offsets_ref[...] - base_ref[0] + SHIFT
    coarse = lax.shift_right_arithmetic(place, 4)
    fine = place - coarse * 16
    coarse = column((coarse * 16).astype(jnp.float32))
    fine = column(fine.astype(jnp.float32))
    lane = lax.broadcasted_iota(jnp.int32, (rows, LANES - HEAD_DIM), 1)
    extra = jnp.where(lane == 0, coarse, jnp.where(lane == 1, fine, 0.0)).astype(jnp.bfloat16)
    for g in range(groups):
        out_ref[:, g * LANES : g * LANES + HEAD_DIM] = query[:, g * HEAD_DIM : (g + 1) * HEAD_DIM]
        out_ref[:, g * LANES + HEAD_DIM : (g + 1) * LANES] = extra


def spread(groups, keys, values, keys_out, values_out):
    count = keys.shape[0]
    lane = lax.broadcasted_iota(jnp.int32, (count, LANES - HEAD_DIM), 1)
    blank = jnp.zeros((count, LANES - HEAD_DIM), jnp.bfloat16)
    ones = jnp.where(lane == 0, 1.0, 0.0).astype(jnp.bfloat16)
    for g in range(groups):
        columns = slice(g * HEAD_DIM, (g + 1) * HEAD_DIM)
        keys_out[g] = jnp.concatenate([keys[:, columns], blank], axis=1)
        values_out[g] = jnp.concatenate([values[:, columns], ones], axis=1)


def block_facts(query, strides, stride, bins, ok):
    extra = query[:, HEAD_DIM:LANES].astype(jnp.float32)
    centre = extra[:, 0:1] + extra[:, 1:2] - (stride * bins + SHIFT).astype(jnp.float32)
    before, after = -centre, centre - float(bins - 1)
    if strides == (0,):
        base = jnp.zeros_like(centre)
    elif min(strides) > 0:
        base = before
    elif max(strides) < 0:
        base = after
    else:
        base = jnp.maximum(before, after)
    return centre, base, (jnp.maximum(before, after) <= RADIUS) & (ok > 0)


def tile_needs(strides, bins, start, size):
    bends, ends = min(strides) <= 0 <= max(strides), False
    for stride in strides:
        low, high = -SHIFT - stride * bins, bins - 1 + SHIFT - stride * bins
        if max(-high, low - (bins - 1)) > RADIUS:
            continue
        if stride >= 0:
            bends |= high > start
            ends |= start + size - 1 - low > RADIUS
        if stride <= 0:
            bends |= low < start + size - 1
            ends |= high - start > RADIUS
    bends |= min(strides) < 0 < max(strides)
    return bends, ends


def attend_rows(blocks, strides, oks, slopes, query_refs, keys_ref, values_ref, out_refs, acc_ref):
    groups, bins, _ = keys_ref.shape
    rows = query_refs[0].shape[0]
    n = len(query_refs)
    parts = [slice(i * rows, (i + 1) * rows) for i in range(n)]
    facts = [block_facts(ref[:, :LANES], block, stride, bins, ok) for ref, block, stride, ok in zip(query_refs, blocks, strides, oks)]
    centre, base = (jnp.concatenate([fact[k] for fact in facts], axis=0) for k in range(2))
    alive = jnp.concatenate([jnp.where(fact[2], 1.0, 0.0) for fact in facts], axis=0) > 0.0

    def queries(g):
        return jnp.concatenate([ref[:, g * LANES : (g + 1) * LANES] for ref in query_refs], axis=0)

    def products(g, start, size):
        keys = keys_ref[g, pl.ds(start, size), :]
        return lax.dot_general(queries(g), keys, OVER_ROWS, preferred_element_type=jnp.float32)

    def positions(start, size):
        return (start + lax.broadcasted_iota(jnp.int32, (1, size), 1)).astype(jnp.float32)

    def finish(g, acc, shift):
        lane = lax.broadcasted_iota(jnp.int32, acc.shape, 1)
        exponent = shift - slopes[g] * base
        coarse = jnp.where(alive, jnp.round(exponent * 0.0625) * 16.0, EMPTY)
        scaled = jnp.where(alive, acc * jnp.exp2(exponent - coarse), 0.0)
        total = scaled[:, HEAD_DIM : HEAD_DIM + 1]
        high = total.astype(jnp.bfloat16).astype(jnp.float32)
        scaled = jnp.where(lane == HEAD_DIM + 1, total - high, scaled)
        scaled = jnp.where(lane == HEAD_DIM + 2, coarse, scaled).astype(jnp.bfloat16)
        for part, ref in zip(parts, out_refs):
            ref[:, g * LANES : (g + 1) * LANES] = scaled[part]

    accs = [jnp.zeros((n * rows, LANES), jnp.float32)] * groups
    for start in range(0, bins, TILE):
        position = positions(start, TILE)
        shapes = []
        for block, (middle, origin, _) in zip(blocks, facts):
            bends, ends = tile_needs(block, bins, start, TILE)
            if bends:
                distance = jnp.abs(position - middle) - origin
            else:
                distance = position if min(block) > 0 else float(bins - 1) - position
            usable = None
            if ends:
                usable = jnp.abs(position - middle) <= RADIUS
            shapes.append((distance, usable))
        for g in range(groups):
            raw = products(g, start, TILE)
            weights = []
            for part, (distance, usable) in zip(parts, shapes):
                weight = jnp.exp2(raw[part] * SCALE2 - slopes[g] * distance)
                weights.append(weight if usable is None else jnp.where(usable, weight, 0.0))
            weights = jnp.concatenate([weight.astype(jnp.bfloat16) for weight in weights], axis=0)
            accs[g] += jnp.dot(weights, values_ref[g, start : start + TILE, :], preferred_element_type=jnp.float32)
    wrong = jnp.zeros((n * rows, 1), jnp.float32)
    for g in range(groups):
        total = accs[g][:, HEAD_DIM : HEAD_DIM + 1]
        wrong = jnp.where((total >= SUM_LO) & (total <= SUM_HI), wrong, 1.0)
        finish(g, accs[g], 0.0)

    @pl.when(jnp.max(jnp.where(alive, wrong, 0.0)) > 0.0)
    def _():
        for g in range(groups):

            def logs(k):
                start = pl.multiple_of(k * LANES, LANES)
                distance = jnp.abs(positions(start, LANES) - centre)
                exponent = products(g, start, LANES) * SCALE2 - slopes[g] * (distance - base)
                return start, jnp.where(distance <= RADIUS, exponent, -FAR)

            def largest(k, so_far):
                return jnp.maximum(so_far, jnp.max(logs(k)[1], axis=1, keepdims=True))

            shift = lax.fori_loop(0, bins // LANES, largest, jnp.full((n * rows, 1), -FAR, jnp.float32))
            acc_ref[...] = jnp.zeros_like(acc_ref)

            @pl.loop(0, bins // LANES)
            def _(k):
                start, exponent = logs(k)
                weights = jnp.exp2(exponent - shift).astype(jnp.bfloat16)
                acc_ref[...] += jnp.dot(weights, values_ref[g, pl.ds(start, LANES), :], preferred_element_type=jnp.float32)

            finish(g, acc_ref[...], shift)


def near_kernel(blocks, slopes_ref, facts_ref, *refs):
    n = len(blocks)
    query_refs, (keys_ref, values_ref, out_ref, acc_ref) = refs[:-4], refs[-4:]
    groups = keys_ref.shape[0]
    rows = out_ref.shape[0] // n
    slices = [pl.ds(i * rows, rows) for i in range(n)]
    if len(query_refs) == 1:
        query_refs = [query_refs[0].at[rows_of] for rows_of in slices]
    attend_rows(
        blocks,
        [facts_ref[2 * i] for i in range(n)],
        [facts_ref[2 * i + 1] for i in range(n)],
        [slopes_ref[g] * LOG2E for g in range(groups)],
        query_refs,
        keys_ref,
        values_ref,
        [out_ref.at[rows_of] for rows_of in slices],
        acc_ref,
    )


def bins_kernel(groups, keys_ref, values_ref, keys_out, values_out):
    spread(groups, keys_ref[...], values_ref[...], keys_out, values_out)


def combined(parts):
    parts = [part.astype(jnp.float32) for part in parts]
    scales = [part[:, HEAD_DIM + 2 : HEAD_DIM + 3] for part in parts]
    top = functools.reduce(jnp.maximum, scales)
    acc = sum(part * jnp.exp2(scale - top) for part, scale in zip(parts, scales))
    return acc, acc[:, HEAD_DIM : HEAD_DIM + 1] + acc[:, HEAD_DIM + 1 : HEAD_DIM + 2], top


def other_kernel(groups, *refs):
    part_refs, out_ref = refs[:-1], refs[-1]
    rows = out_ref.shape[0]
    lane = lax.broadcasted_iota(jnp.int32, (rows, LANES), 1)
    for g in range(groups):
        lanes = slice(g * LANES, (g + 1) * LANES)
        acc, total, top = combined([ref[rows:, lanes] for ref in part_refs])
        high = total.astype(jnp.bfloat16).astype(jnp.float32)
        acc = jnp.where(lane == HEAD_DIM, high, jnp.where(lane == HEAD_DIM + 1, total - high, acc))
        acc = jnp.where(lane == HEAD_DIM + 2, top, acc)
        out_ref[:, lanes] = acc.astype(jnp.bfloat16)


def merge_kernel(groups, place_ref, *refs):
    part_refs, (w_ref, keep_ref, send_ref) = refs[:-3], refs[-3:]
    rows = part_refs[0].shape[0]
    pooled = []
    for g in range(groups):
        acc, total, _ = combined([ref[:rows, g * LANES : (g + 1) * LANES] for ref in part_refs])
        pooled.append((acc[:, :HEAD_DIM] / total).astype(jnp.bfloat16))
    width = w_ref.shape[1] // 4
    core, high = place_ref[0] & 1, place_ref[0] >> 1
    for k in range(2):
        row = jnp.where(k == 0, high, 1 - high) * 2
        for ref, lane in ((send_ref, 1 - core), (keep_ref, core)):
            start = pl.multiple_of((row + lane) * width, LANES)
            acc = jnp.zeros((rows, width), jnp.float32)
            for g in range(groups):
                weights = w_ref[g * HEAD_DIM : (g + 1) * HEAD_DIM, pl.ds(start, width)]
                acc += jnp.dot(pooled[g], weights, preferred_element_type=jnp.float32)
            ref[k] = acc.astype(ref.dtype)


def attend_cost(rows, bins, groups):
    return pl.CostEstimate(
        flops=4 * rows * bins * groups * LANES, bytes_accessed=4 * 2**20, transcendentals=rows * bins * groups
    )


def prepare_queries(queries, cell_types, promoters, offsets, cell_embed, base, groups):
    rows = queries.shape[0]
    sources = [cell_types[None, :], promoters[None, :], offsets[None, :], queries, cell_embed]
    return pl.pallas_call(
        functools.partial(query_kernel, groups),
        in_specs=[SMEM] + [HBM] * 5,
        out_specs=VMEM,
        out_shape=jax.ShapeDtypeStruct((rows, groups * LANES), jnp.bfloat16),
        scratch_shapes=[pltpu.VMEM(a.shape, a.dtype) for a in sources] + [pltpu.SemaphoreType.DMA((5,))],
        compiler_params=pltpu.CompilerParams(vmem_limit_bytes=QUERY_VMEM),
        name="prepare_queries",
    )(base[None], *sources)


def prepare_bins(keys, values, groups):
    bins = keys.shape[0]
    step = 256
    flat = pl.BlockSpec((step, keys.shape[1]), lambda i: (i, 0))
    split = pl.BlockSpec((groups, step, LANES), lambda i: (0, i, 0))
    return pl.pallas_call(
        functools.partial(bins_kernel, groups),
        grid=(bins // step,),
        in_specs=[flat, flat],
        out_specs=[split, split],
        out_shape=[jax.ShapeDtypeStruct((groups, bins, LANES), jnp.bfloat16)] * 2,
        compiler_params=pltpu.CompilerParams(vmem_limit_bytes=BINS_VMEM),
        cost_estimate=pl.CostEstimate(flops=0, bytes_accessed=7 * 2**20, transcendentals=0),
        name="prepare_bins",
    )(keys, values)


def attend_near(blocks, slopes, facts, queries, keys, values):
    groups, bins, _ = keys.shape
    width = queries[0].shape[1]
    rows = sum(query.shape[0] for query in queries)
    return pl.pallas_call(
        functools.partial(near_kernel, blocks),
        in_specs=[SMEM, SMEM] + [VMEM] * (len(queries) + 2),
        out_specs=VMEM,
        out_shape=jax.ShapeDtypeStruct((rows, width), jnp.bfloat16),
        scratch_shapes=[pltpu.VMEM((rows, LANES), jnp.float32)],
        compiler_params=pltpu.CompilerParams(vmem_limit_bytes=24 * 2**20),
        cost_estimate=attend_cost(rows, bins, groups),
        name="attend_near",
    )(slopes, facts, *queries, keys, values)


def merge_other(parts, groups):
    rows, width = parts[0].shape
    return pl.pallas_call(
        functools.partial(other_kernel, groups),
        in_specs=[VMEM] * len(parts),
        out_specs=VMEM,
        out_shape=jax.ShapeDtypeStruct((rows // 2, width), jnp.bfloat16),
        compiler_params=pltpu.CompilerParams(vmem_limit_bytes=8 * 2**20),
        name="merge_other",
    )(*parts)


def merge(place, parts, w_out, groups):
    rows = parts[0].shape[0]
    width = w_out.shape[1] // 4
    return pl.pallas_call(
        functools.partial(merge_kernel, groups),
        in_specs=[SMEM] + [VMEM] * (len(parts) + 1),
        out_specs=[VMEM] * 2,
        out_shape=[
            jax.ShapeDtypeStruct((2, rows, width), jnp.float32),
            jax.ShapeDtypeStruct((2, rows, width), jnp.bfloat16),
        ],
        compiler_params=pltpu.CompilerParams(vmem_limit_bytes=12 * 2**20),
        name="merge",
    )(place[None], *parts, w_out)


def rotated(value, steps):
    count = lax.axis_size("seq")
    return lax.ppermute(value, "seq", [(i, (i + steps) % count) for i in range(count)])


def swapped(value, axis, bit):
    return lax.ppermute(value, axis, [(i, i ^ bit) for i in range(lax.axis_size(axis))])


def local(queries, cell_types, promoters, offsets, cell_embed, bin_keys, bin_values, slopes, w_out):
    seq_count = lax.axis_size("seq")
    position = lax.axis_index("seq")
    place = lax.axis_index("head")
    bins = bin_keys.shape[0]
    groups = slopes.shape[0]
    odd = position & 1

    def facts(pairs):
        found = []
        for shift, same in pairs:
            stride = 2 * shift if same else 2 * shift + 2 * odd - 1
            block = position - stride
            found += [stride + 0 * odd, ((block >= 0) & (block < seq_count)).astype(jnp.int32)]
        return jnp.stack(found).astype(jnp.int32)

    mine = prepare_queries(queries, cell_types, promoters, offsets, cell_embed, position * bins, groups)
    other = swapped(mine, "seq", 1)
    keys, values = prepare_bins(bin_keys, bin_values, groups)
    other, keys, values = lax.optimization_barrier((other, keys, values))
    both = jnp.concatenate([mine, other], axis=0)
    shifts = [2, -2, 1, -1]
    arrived = [rotated(both, 2 * shift) for shift in shifts]
    part = attend_near(
        ((0,), (-1, 1)), slopes, facts([(0, True), (0, False)]), [mine, other], keys, values
    )
    parts = [part]
    for k in (2, 3, 0, 1):
        shift = shifts[k]
        query, _ = lax.optimization_barrier((arrived[k], part))
        part = attend_near(
            ((2 * shift,), (2 * shift - 1, 2 * shift + 1)), slopes, facts([(shift, True), (shift, False)]), [query], keys, values
        )
        parts.append(rotated(part, -2 * shift))
    theirs = swapped(merge_other(parts, groups), "seq", 1)
    keep, send = merge(place, [theirs] + parts, w_out, groups)
    got = swapped(send, "head", 1)
    rest = (keep[1] + got[1].astype(jnp.float32)).astype(jnp.bfloat16)
    last = swapped(rest, "head", 2)
    return (keep[0] + got[0].astype(jnp.float32) + last.astype(jnp.float32)).astype(jnp.bfloat16)


def solution(mesh):
    return jax.shard_map(
        local,
        mesh=mesh,
        in_specs=(
            P("seq", "head"),
            P("seq"),
            P("seq"),
            P("seq"),
            P(None, "head"),
            P("seq", "head"),
            P("seq", "head"),
            P("head"),
            P("head", None),
        ),
        out_specs=P("seq", "head"),
        check_vma=False,
    )
```

```python
import functools
import math

import jax
import jax.numpy as jnp
from jax import lax
from jax.experimental import pallas as pl
from jax.experimental.pallas import tpu as pltpu
from jax.sharding import PartitionSpec as P

HEAD_DIM = 96
RADIUS = 7812
SHIFT = 64
LANES = 128
LOG2E = math.log2(math.e)
SCALE2 = LOG2E / math.sqrt(HEAD_DIM)
FAR = 1e30
EMPTY = -16384.0
SUM_LO, SUM_HI = 2.0**-60, 2.0**100
TILE = 512
ORDER = (2, 3, 0, 1)
QUERY_VMEM = 4 * 2**20
EXTRA = 16

SMEM = pl.BlockSpec(memory_space=pltpu.SMEM)
VMEM = pl.BlockSpec(memory_space=pltpu.VMEM)
HBM = pl.BlockSpec(memory_space=pltpu.HBM)


def query_kernel(base_ref, *refs):
    sources, out_ref, copies, sems = refs[:5], refs[5], refs[6:11], refs[11]
    moves = [pltpu.make_async_copy(a, b, sems.at[i]) for i, (a, b) in enumerate(zip(sources, copies))]
    for move in moves:
        move.start()
    for move in moves:
        move.wait()
    types_ref, promoters_ref, offsets_ref, queries_ref, embed_ref = copies
    rows, width = queries_ref.shape
    kinds = embed_ref.shape[0]
    one_hot = (lax.broadcasted_iota(jnp.int32, (kinds, rows), 0) == types_ref[...]).astype(jnp.float32)
    embedded = jnp.dot(one_hot.T.astype(jnp.bfloat16), embed_ref[...], preferred_element_type=jnp.float32)
    query = queries_ref[...].astype(jnp.float32) + embedded
    out_ref[:width, :] = query.T.astype(jnp.bfloat16)
    place = promoters_ref[...] + offsets_ref[...] - base_ref[0] + SHIFT
    coarse = lax.shift_right_arithmetic(place, 4) * 16
    line = lax.broadcasted_iota(jnp.int32, (EXTRA, rows), 0)
    extra = jnp.where(line == 0, coarse, jnp.where(line == 1, place - coarse, 0))
    out_ref[width:, :] = extra.astype(jnp.float32).astype(jnp.bfloat16)


def bins_kernel(values_ref, out_ref):
    groups, _, bins = out_ref.shape
    values = values_ref[...].T
    for g in range(groups):
        out_ref[g, :HEAD_DIM, :] = values[g * HEAD_DIM : (g + 1) * HEAD_DIM]
        out_ref[g, HEAD_DIM:, :] = jnp.ones((EXTRA, bins), jnp.bfloat16)


def block_facts(extra, strides, stride, bins, ok):
    extra = extra.astype(jnp.float32)
    centre = extra[0:1] + extra[1:2] - (stride * bins + SHIFT).astype(jnp.float32)
    before, after = -centre, centre - float(bins - 1)
    if strides == (0,):
        base = jnp.zeros_like(centre)
    elif min(strides) > 0:
        base = before
    elif max(strides) < 0:
        base = after
    else:
        base = jnp.maximum(before, after)
    alive = jnp.where(jnp.maximum(before, after) <= RADIUS, 1.0, 0.0) * jnp.where(ok, 1.0, 0.0)
    return centre, base, alive


def tile_needs(strides, bins, start, size):
    bends, ends = min(strides) <= 0 <= max(strides), False
    for stride in strides:
        low, high = -SHIFT - stride * bins, bins - 1 + SHIFT - stride * bins
        if max(-high, low - (bins - 1)) > RADIUS:
            continue
        if stride >= 0:
            bends |= high > start
            ends |= start + size - 1 - low > RADIUS
        if stride <= 0:
            bends |= low < start + size - 1
            ends |= high - start > RADIUS
    return bends, ends


def attend_rows(blocks, strides, oks, slopes, query_refs, keys_ref, values_ref, out_refs, acc_ref):
    bins, width = keys_ref.shape
    groups = values_ref.shape[0]
    rows = query_refs[0].shape[1]
    n = len(query_refs)
    parts = [slice(i * rows, (i + 1) * rows) for i in range(n)]
    facts = [block_facts(ref[width:, :], *each, bins, ok) for ref, *each, ok in zip(query_refs, blocks, strides, oks)]
    centre, base, alive = (jnp.concatenate([fact[k] for fact in facts], axis=1) for k in range(3))
    alive = alive > 0.0
    windows, queries = [], []
    for g in range(groups):
        low, high = g * HEAD_DIM, (g + 1) * HEAD_DIM
        first, last = low // LANES * LANES, -(-high // LANES) * LANES
        query = jnp.concatenate([ref[low:high, :] for ref in query_refs], axis=1)
        pads = [jnp.zeros((size, n * rows), jnp.bfloat16) for size in (low - first, last - high)]
        pieces = [piece for piece in (pads[0], query, pads[1]) if piece.shape[0]]
        windows.append(slice(first, last))
        queries.append(jnp.concatenate(pieces, axis=0))

    def products(g, start, size):
        return jnp.dot(keys_ref[pl.ds(start, size), windows[g]], queries[g], preferred_element_type=jnp.float32)

    def positions(start, size):
        return (start + lax.broadcasted_iota(jnp.int32, (size, 1), 0)).astype(jnp.float32)

    line = lax.broadcasted_iota(jnp.int32, (EXTRA, n * rows), 0)

    def finish(g, acc, shift, extra):
        exponent = shift - slopes[g] * base
        coarse = jnp.where(alive, jnp.round(exponent * 0.0625) * 16.0, EMPTY)
        factor = jnp.where(alive, jnp.exp2(exponent - coarse), 0.0)
        scaled = jnp.where(alive, acc * factor, 0.0)
        total = scaled[HEAD_DIM : HEAD_DIM + 1]
        high = total.astype(jnp.bfloat16).astype(jnp.float32)
        for part, ref in zip(parts, out_refs):
            ref[g * HEAD_DIM : (g + 1) * HEAD_DIM, :] = scaled[:HEAD_DIM, part].astype(jnp.bfloat16)
        for k, row in enumerate((high, total - high, coarse)):
            extra = jnp.where(line == k * groups + g, row, extra)
        return extra

    def finished(extra):
        for part, ref in zip(parts, out_refs):
            ref[width:, :] = extra[:, part].astype(jnp.bfloat16)

    accs = [None] * groups
    for start in range(0, bins, TILE):
        position = positions(start, TILE)
        shapes = []
        for block, (middle, origin, _) in zip(blocks, facts):
            bends, ends = tile_needs(block, bins, start, TILE)
            if bends:
                distance = jnp.abs(position - middle) - origin
            else:
                distance = position if min(block) > 0 else float(bins - 1) - position
            shapes.append((distance, jnp.abs(position - middle) <= RADIUS if ends else None))
        weights = []
        for g in range(groups):
            raw = products(g, start, TILE)
            pieces = []
            for part, (distance, usable) in zip(parts, shapes):
                weight = jnp.exp2(raw[:, part] * SCALE2 - slopes[g] * distance)
                weight = weight if usable is None else jnp.where(usable, weight, 0.0)
                pieces.append(weight.astype(jnp.bfloat16))
            weights.append(jnp.concatenate(pieces, axis=1))
        for g in range(groups):
            gained = jnp.dot(values_ref[g, :, start : start + TILE], weights[g], preferred_element_type=jnp.float32)
            accs[g] = gained if accs[g] is None else accs[g] + gained
    wrong = jnp.zeros((1, n * rows), jnp.float32)
    extra = jnp.zeros((EXTRA, n * rows), jnp.float32)
    for g in range(groups):
        total = accs[g][HEAD_DIM : HEAD_DIM + 1]
        wrong = jnp.where((total >= SUM_LO) & (total <= SUM_HI), wrong, 1.0)
        extra = finish(g, accs[g], 0.0, extra)
    finished(extra)

    @pl.when(jnp.max(jnp.where(alive, wrong, 0.0)) > 0.0)
    def _():
        extra = jnp.zeros((EXTRA, n * rows), jnp.float32)
        for g in range(groups):

            def logs(k):
                start = pl.multiple_of(k * LANES, LANES)
                distance = jnp.abs(positions(start, LANES) - centre)
                exponent = products(g, start, LANES) * SCALE2 - slopes[g] * (distance - base)
                return start, jnp.where(distance <= RADIUS, exponent, -FAR)

            def largest(k, so_far):
                return jnp.maximum(so_far, jnp.max(logs(k)[1], axis=0, keepdims=True))

            shift = lax.fori_loop(0, bins // LANES, largest, jnp.full((1, n * rows), -FAR, jnp.float32))
            acc_ref[...] = jnp.zeros_like(acc_ref)

            @pl.loop(0, bins // LANES)
            def _(k):
                start, exponent = logs(k)
                weights = jnp.exp2(exponent - shift).astype(jnp.bfloat16)
                acc_ref[...] += jnp.dot(values_ref[g, :, pl.ds(start, LANES)], weights, preferred_element_type=jnp.float32)

            extra = finish(g, acc_ref[...], shift, extra)
        finished(extra)


def near_kernel(shifts, seq_count, slopes_ref, position_ref, *refs):
    query_refs, (keys_ref, values_ref, out_ref, acc_ref) = refs[:-4], refs[-4:]
    if len(query_refs) == 1:
        query_refs = [query_refs[0].at[i] for i in range(len(shifts))]
    position = position_ref[0]
    odd = position & 1
    blocks, strides, oks = [], [], []
    for shift, same in shifts:
        block = (2 * shift,) if same else (2 * shift - 1, 2 * shift + 1)
        stride = jnp.int32(2 * shift) if same else 2 * shift + 2 * odd - 1
        blocks.append(block)
        strides.append(stride)
        oks.append((position - stride >= 0) & (position - stride < seq_count))
    attend_rows(
        blocks,
        strides,
        oks,
        [slopes_ref[g] * LOG2E for g in range(values_ref.shape[0])],
        query_refs,
        keys_ref,
        values_ref,
        [out_ref.at[i] for i in range(len(shifts))],
        acc_ref,
    )


def combined(groups, refs):
    width = groups * HEAD_DIM
    extras = [ref[width:, :].astype(jnp.float32) for ref in refs]
    found = []
    for g in range(groups):
        scales = [extra[2 * groups + g : 2 * groups + g + 1] for extra in extras]
        top = functools.reduce(jnp.maximum, scales)
        acc, total = 0.0, 0.0
        for ref, extra, scale in zip(refs, extras, scales):
            factor = jnp.exp2(scale - top)
            acc += ref[g * HEAD_DIM : (g + 1) * HEAD_DIM, :].astype(jnp.float32) * factor
            total += (extra[g : g + 1] + extra[groups + g : groups + g + 1]) * factor
        found.append((acc, total, top))
    return found


def other_kernel(groups, *refs):
    part_refs, out_ref = refs[:-1], refs[-1]
    width = groups * HEAD_DIM
    line = lax.broadcasted_iota(jnp.int32, (EXTRA, out_ref.shape[1]), 0)
    extra = jnp.zeros(line.shape, jnp.float32)
    for g, (acc, total, top) in enumerate(combined(groups, [ref.at[1] for ref in part_refs])):
        high = total.astype(jnp.bfloat16).astype(jnp.float32)
        for k, row in enumerate((high, total - high, top)):
            extra = jnp.where(line == k * groups + g, row, extra)
        out_ref[g * HEAD_DIM : (g + 1) * HEAD_DIM, :] = acc.astype(jnp.bfloat16)
    out_ref[width:, :] = extra.astype(jnp.bfloat16)


def merge_kernel(groups, place_ref, theirs_ref, *refs):
    part_refs, (w_ref, keep_ref, send_ref) = refs[:-3], refs[-3:]
    shares = combined(groups, [theirs_ref] + [ref.at[0] for ref in part_refs])
    pooled = jnp.concatenate([acc / total for acc, total, _ in shares], axis=0).T.astype(jnp.bfloat16)
    width = w_ref.shape[1] // 4
    core, high = place_ref[0] & 1, place_ref[0] >> 1
    for k in range(2):
        row = (high if k == 0 else 1 - high) * 2
        for ref, lane in ((send_ref, 1 - core), (keep_ref, core)):
            start = pl.multiple_of((row + lane) * width, LANES)
            ref[k] = jnp.dot(pooled, w_ref[:, pl.ds(start, width)], preferred_element_type=jnp.float32).astype(ref.dtype)


def prepare_queries(queries, cell_types, promoters, offsets, cell_embed, base):
    rows, width = queries.shape
    sources = [cell_types[None, :], promoters[None, :], offsets[None, :], queries, cell_embed]
    return pl.pallas_call(
        query_kernel,
        in_specs=[SMEM] + [HBM] * 5,
        out_specs=VMEM,
        out_shape=jax.ShapeDtypeStruct((width + EXTRA, rows), jnp.bfloat16),
        scratch_shapes=[pltpu.VMEM(a.shape, a.dtype) for a in sources] + [pltpu.SemaphoreType.DMA((5,))],
        compiler_params=pltpu.CompilerParams(vmem_limit_bytes=QUERY_VMEM),
        name="prepare_queries",
    )(base[None], *sources)


def prepare_bins(values, groups):
    bins = values.shape[0]
    return pl.pallas_call(
        bins_kernel,
        in_specs=[VMEM],
        out_specs=VMEM,
        out_shape=jax.ShapeDtypeStruct((groups, HEAD_DIM + EXTRA, bins), jnp.bfloat16),
        compiler_params=pltpu.CompilerParams(vmem_limit_bytes=16 * 2**20),
        cost_estimate=pl.CostEstimate(flops=0, bytes_accessed=4 * 2**20, transcendentals=0),
        name="prepare_bins",
    )(values)


def attend_near(shifts, seq_count, slopes, position, queries, keys, values):
    groups, depth, bins = values.shape
    n = len(shifts)
    height, rows = queries[0].shape[-2:]
    return pl.pallas_call(
        functools.partial(near_kernel, shifts, seq_count),
        in_specs=[SMEM, SMEM] + [VMEM] * (len(queries) + 2),
        out_specs=VMEM,
        out_shape=jax.ShapeDtypeStruct((n, height, rows), jnp.bfloat16),
        scratch_shapes=[pltpu.VMEM((depth, n * rows), jnp.float32)],
        compiler_params=pltpu.CompilerParams(vmem_limit_bytes=24 * 2**20),
        cost_estimate=pl.CostEstimate(
            flops=4 * n * rows * bins * groups * LANES, bytes_accessed=4 * 2**20, transcendentals=n * rows * bins * groups
        ),
        name="attend_near",
    )(slopes, position[None], *queries, keys, values)


def merge_other(parts, groups):
    return pl.pallas_call(
        functools.partial(other_kernel, groups),
        in_specs=[VMEM] * len(parts),
        out_specs=VMEM,
        out_shape=jax.ShapeDtypeStruct(parts[0].shape[1:], jnp.bfloat16),
        compiler_params=pltpu.CompilerParams(vmem_limit_bytes=8 * 2**20),
        name="merge_other",
    )(*parts)


def merge(place, theirs, parts, w_out, groups):
    rows = theirs.shape[1]
    width = w_out.shape[1] // 4
    return pl.pallas_call(
        functools.partial(merge_kernel, groups),
        in_specs=[SMEM] + [VMEM] * (len(parts) + 2),
        out_specs=[VMEM] * 2,
        out_shape=[
            jax.ShapeDtypeStruct((2, rows, width), jnp.float32),
            jax.ShapeDtypeStruct((2, rows, width), jnp.bfloat16),
        ],
        compiler_params=pltpu.CompilerParams(vmem_limit_bytes=12 * 2**20),
        name="merge",
    )(place[None], theirs, *parts, w_out)


def rotated(value, steps):
    count = lax.axis_size("seq")
    return lax.ppermute(value, "seq", [(i, (i + steps) % count) for i in range(count)])


def swapped(value, axis, bit):
    return lax.ppermute(value, axis, [(i, i ^ bit) for i in range(lax.axis_size(axis))])


def local(queries, cell_types, promoters, offsets, cell_embed, bin_keys, bin_values, slopes, w_out):
    seq_count = lax.axis_size("seq")
    position = lax.axis_index("seq")
    place = lax.axis_index("head")
    bins = bin_keys.shape[0]
    groups = slopes.shape[0]

    mine = prepare_queries(queries, cell_types, promoters, offsets, cell_embed, position * bins)
    other = swapped(mine, "seq", 1)
    values = prepare_bins(bin_values, groups)
    other, values = lax.optimization_barrier((other, values))
    both = jnp.stack([mine, other])
    shifts = [2, -2, 1, -1]
    arrived = [rotated(both, 2 * shift) for shift in shifts]
    part = attend_near(((0, True), (0, False)), seq_count, slopes, position, [mine, other], bin_keys, values)
    parts = [part]
    for k in ORDER:
        shift = shifts[k]
        query = arrived[k]
        if k == ORDER[0]:
            query, _ = lax.optimization_barrier((query, part))
        share = attend_near(((shift, True), (shift, False)), seq_count, slopes, position, [query], bin_keys, values)
        parts.append(rotated(share, -2 * shift))
    theirs = swapped(merge_other(parts, groups), "seq", 1)
    keep, send = merge(place, theirs, parts, w_out, groups)
    got = swapped(send, "head", 1)
    rest = (keep[1] + got[1].astype(jnp.float32)).astype(jnp.bfloat16)
    last = swapped(rest, "head", 2)
    return (keep[0] + got[0].astype(jnp.float32) + last.astype(jnp.float32)).astype(jnp.bfloat16)


def solution(mesh):
    return jax.shard_map(
        local,
        mesh=mesh,
        in_specs=(
            P("seq", "head"),
            P("seq"),
            P("seq"),
            P("seq"),
            P(None, "head"),
            P("seq", "head"),
            P("seq", "head"),
            P("head"),
            P("head", None),
        ),
        out_specs=P("seq", "head"),
        check_vma=False,
    )
```

```python
import functools
import math

import jax
import jax.numpy as jnp
from jax import lax
from jax.experimental import pallas as pl
from jax.experimental.pallas import tpu as pltpu
from jax.sharding import PartitionSpec as P

HEAD_DIM = 96
RADIUS = 7812
SHIFT = 64
LANES = 128
LOG2E = math.log2(math.e)
SCALE2 = LOG2E / math.sqrt(HEAD_DIM)
FAR = 1e30
EMPTY = -16384.0
SUM_LO, SUM_HI = 2.0**-60, 2.0**100
TILE = 512
ORDER = (2, 3, 0, 1)
QUERY_VMEM = 60 * 2**20
EXTRA = 16

SMEM = pl.BlockSpec(memory_space=pltpu.SMEM)
VMEM = pl.BlockSpec(memory_space=pltpu.VMEM)
HBM = pl.BlockSpec(memory_space=pltpu.HBM)


def query_kernel(base_ref, *refs):
    sources, out_ref, copies, sems = refs[:5], refs[5], refs[6:11], refs[11]
    moves = [pltpu.make_async_copy(a, b, sems.at[i]) for i, (a, b) in enumerate(zip(sources, copies))]
    for move in moves:
        move.start()
    for move in moves:
        move.wait()
    types_ref, promoters_ref, offsets_ref, queries_ref, embed_ref = copies
    rows, width = queries_ref.shape
    kinds = embed_ref.shape[0]
    one_hot = (lax.broadcasted_iota(jnp.int32, (kinds, rows), 0) == types_ref[...]).astype(jnp.float32)
    embedded = jnp.dot(one_hot.T.astype(jnp.bfloat16), embed_ref[...], preferred_element_type=jnp.float32)
    query = queries_ref[...].astype(jnp.float32) + embedded
    out_ref[:width, :] = query.T.astype(jnp.bfloat16)
    place = promoters_ref[...] + offsets_ref[...] - base_ref[0] + SHIFT
    coarse = lax.shift_right_arithmetic(place, 4) * 16
    line = lax.broadcasted_iota(jnp.int32, (EXTRA, rows), 0)
    extra = jnp.where(line == 0, coarse, jnp.where(line == 1, place - coarse, 0))
    out_ref[width:, :] = extra.astype(jnp.float32).astype(jnp.bfloat16)


def bins_kernel(values_ref, out_ref):
    groups, _, bins = out_ref.shape
    values = values_ref[...].T
    for g in range(groups):
        out_ref[g, :HEAD_DIM, :] = values[g * HEAD_DIM : (g + 1) * HEAD_DIM]
        out_ref[g, HEAD_DIM:, :] = jnp.ones((EXTRA, bins), jnp.bfloat16)


def block_facts(extra, strides, stride, bins, ok):
    extra = extra.astype(jnp.float32)
    centre = extra[0:1] + extra[1:2] - (stride * bins + SHIFT).astype(jnp.float32)
    before, after = -centre, centre - float(bins - 1)
    if strides == (0,):
        base = jnp.zeros_like(centre)
    elif min(strides) > 0:
        base = before
    elif max(strides) < 0:
        base = after
    else:
        base = jnp.maximum(before, after)
    alive = jnp.where(jnp.maximum(before, after) <= RADIUS, 1.0, 0.0) * jnp.where(ok, 1.0, 0.0)
    return centre, base, alive


def tile_needs(strides, bins, start, size):
    bends, ends = min(strides) <= 0 <= max(strides), False
    for stride in strides:
        low, high = -SHIFT - stride * bins, bins - 1 + SHIFT - stride * bins
        if max(-high, low - (bins - 1)) > RADIUS:
            continue
        if stride >= 0:
            bends |= high > start
            ends |= start + size - 1 - low > RADIUS
        if stride <= 0:
            bends |= low < start + size - 1
            ends |= high - start > RADIUS
    return bends, ends


def attend_rows(blocks, strides, oks, slopes, query_refs, keys_ref, values_ref, out_refs, acc_ref):
    bins, width = keys_ref.shape
    groups = values_ref.shape[0]
    rows = query_refs[0].shape[1]
    n = len(query_refs)
    parts = [slice(i * rows, (i + 1) * rows) for i in range(n)]
    facts = [block_facts(ref[width:, :], *each, bins, ok) for ref, *each, ok in zip(query_refs, blocks, strides, oks)]
    centre, base, alive = (jnp.concatenate([fact[k] for fact in facts], axis=1) for k in range(3))
    alive = alive > 0.0
    windows, queries = [], []
    for g in range(groups):
        low, high = g * HEAD_DIM, (g + 1) * HEAD_DIM
        first, last = low // LANES * LANES, -(-high // LANES) * LANES
        query = jnp.concatenate([ref[low:high, :] for ref in query_refs], axis=1)
        pads = [jnp.zeros((size, n * rows), jnp.bfloat16) for size in (low - first, last - high)]
        pieces = [piece for piece in (pads[0], query, pads[1]) if piece.shape[0]]
        windows.append(slice(first, last))
        queries.append(jnp.concatenate(pieces, axis=0))

    def products(g, start, size):
        return jnp.dot(keys_ref[pl.ds(start, size), windows[g]], queries[g], preferred_element_type=jnp.float32)

    def positions(start, size):
        return (start + lax.broadcasted_iota(jnp.int32, (size, 1), 0)).astype(jnp.float32)

    line = lax.broadcasted_iota(jnp.int32, (EXTRA, n * rows), 0)

    def finish(g, acc, shift, extra):
        exponent = shift - slopes[g] * base
        coarse = jnp.where(alive, jnp.round(exponent * 0.0625) * 16.0, EMPTY)
        factor = jnp.where(alive, jnp.exp2(exponent - coarse), 0.0)
        scaled = jnp.where(alive, acc * factor, 0.0)
        total = scaled[HEAD_DIM : HEAD_DIM + 1]
        high = total.astype(jnp.bfloat16).astype(jnp.float32)
        for part, ref in zip(parts, out_refs):
            ref[g * HEAD_DIM : (g + 1) * HEAD_DIM, :] = scaled[:HEAD_DIM, part].astype(jnp.bfloat16)
        for k, row in enumerate((high, total - high, coarse)):
            extra = jnp.where(line == k * groups + g, row, extra)
        return extra

    def finished(extra):
        for part, ref in zip(parts, out_refs):
            ref[width:, :] = extra[:, part].astype(jnp.bfloat16)

    accs = [None] * groups
    for start in range(0, bins, TILE):
        position = positions(start, TILE)
        shapes = []
        for block, (middle, origin, _) in zip(blocks, facts):
            bends, ends = tile_needs(block, bins, start, TILE)
            if bends:
                distance = jnp.abs(position - middle) - origin
            else:
                distance = position if min(block) > 0 else float(bins - 1) - position
            shapes.append((distance, jnp.abs(position - middle) <= RADIUS if ends else None))
        weights = []
        for g in range(groups):
            raw = products(g, start, TILE)
            pieces = []
            for part, (distance, usable) in zip(parts, shapes):
                weight = jnp.exp2(raw[:, part] * SCALE2 - slopes[g] * distance)
                weight = weight if usable is None else jnp.where(usable, weight, 0.0)
                pieces.append(weight.astype(jnp.bfloat16))
            weights.append(jnp.concatenate(pieces, axis=1))
        for g in range(groups):
            gained = jnp.dot(values_ref[g, :, start : start + TILE], weights[g], preferred_element_type=jnp.float32)
            accs[g] = gained if accs[g] is None else accs[g] + gained
    wrong = jnp.zeros((1, n * rows), jnp.float32)
    extra = jnp.zeros((EXTRA, n * rows), jnp.float32)
    for g in range(groups):
        total = accs[g][HEAD_DIM : HEAD_DIM + 1]
        wrong = jnp.where((total >= SUM_LO) & (total <= SUM_HI), wrong, 1.0)
        extra = finish(g, accs[g], 0.0, extra)
    finished(extra)

    @pl.when(jnp.max(jnp.where(alive, wrong, 0.0)) > 0.0)
    def _():
        extra = jnp.zeros((EXTRA, n * rows), jnp.float32)
        for g in range(groups):

            def logs(k):
                start = pl.multiple_of(k * LANES, LANES)
                distance = jnp.abs(positions(start, LANES) - centre)
                exponent = products(g, start, LANES) * SCALE2 - slopes[g] * (distance - base)
                return start, jnp.where(distance <= RADIUS, exponent, -FAR)

            def largest(k, so_far):
                return jnp.maximum(so_far, jnp.max(logs(k)[1], axis=0, keepdims=True))

            shift = lax.fori_loop(0, bins // LANES, largest, jnp.full((1, n * rows), -FAR, jnp.float32))
            acc_ref[...] = jnp.zeros_like(acc_ref)

            @pl.loop(0, bins // LANES)
            def _(k):
                start, exponent = logs(k)
                weights = jnp.exp2(exponent - shift).astype(jnp.bfloat16)
                acc_ref[...] += jnp.dot(values_ref[g, :, pl.ds(start, LANES)], weights, preferred_element_type=jnp.float32)

            extra = finish(g, acc_ref[...], shift, extra)
        finished(extra)


def near_kernel(shifts, seq_count, slopes_ref, position_ref, *refs):
    query_refs, (keys_ref, values_ref, out_ref, acc_ref) = refs[:-4], refs[-4:]
    if len(query_refs) == 1:
        query_refs = [query_refs[0].at[i] for i in range(len(shifts))]
    position = position_ref[0]
    odd = position & 1
    blocks, strides, oks = [], [], []
    for shift, same in shifts:
        block = (2 * shift,) if same else (2 * shift - 1, 2 * shift + 1)
        stride = jnp.int32(2 * shift) if same else 2 * shift + 2 * odd - 1
        blocks.append(block)
        strides.append(stride)
        oks.append((position - stride >= 0) & (position - stride < seq_count))
    attend_rows(
        blocks,
        strides,
        oks,
        [slopes_ref[g] * LOG2E for g in range(values_ref.shape[0])],
        query_refs,
        keys_ref,
        values_ref,
        [out_ref.at[i] for i in range(len(shifts))],
        acc_ref,
    )


def combined(groups, refs):
    width = groups * HEAD_DIM
    extras = [ref[width:, :].astype(jnp.float32) for ref in refs]
    found = []
    for g in range(groups):
        scales = [extra[2 * groups + g : 2 * groups + g + 1] for extra in extras]
        top = functools.reduce(jnp.maximum, scales)
        acc, total = 0.0, 0.0
        for ref, extra, scale in zip(refs, extras, scales):
            factor = jnp.exp2(scale - top)
            acc += ref[g * HEAD_DIM : (g + 1) * HEAD_DIM, :].astype(jnp.float32) * factor
            total += (extra[g : g + 1] + extra[groups + g : groups + g + 1]) * factor
        found.append((acc, total, top))
    return found


def other_kernel(groups, *refs):
    part_refs, out_ref = refs[:-1], refs[-1]
    width = groups * HEAD_DIM
    line = lax.broadcasted_iota(jnp.int32, (EXTRA, out_ref.shape[1]), 0)
    extra = jnp.zeros(line.shape, jnp.float32)
    for g, (acc, total, top) in enumerate(combined(groups, [ref.at[1] for ref in part_refs])):
        high = total.astype(jnp.bfloat16).astype(jnp.float32)
        for k, row in enumerate((high, total - high, top)):
            extra = jnp.where(line == k * groups + g, row, extra)
        out_ref[g * HEAD_DIM : (g + 1) * HEAD_DIM, :] = acc.astype(jnp.bfloat16)
    out_ref[width:, :] = extra.astype(jnp.bfloat16)


def merge_kernel(groups, place_ref, theirs_ref, *refs):
    part_refs, (w_ref, keep_ref, send_ref) = refs[:-3], refs[-3:]
    shares = combined(groups, [theirs_ref] + [ref.at[0] for ref in part_refs])
    pooled = jnp.concatenate([acc / total for acc, total, _ in shares], axis=0).T.astype(jnp.bfloat16)
    width = w_ref.shape[1] // 4
    core, high = place_ref[0] & 1, place_ref[0] >> 1
    for k in range(2):
        row = (high if k == 0 else 1 - high) * 2
        for ref, lane in ((send_ref, 1 - core), (keep_ref, core)):
            start = pl.multiple_of((row + lane) * width, LANES)
            ref[k] = jnp.dot(pooled, w_ref[:, pl.ds(start, width)], preferred_element_type=jnp.float32).astype(ref.dtype)


def prepare_queries(queries, cell_types, promoters, offsets, cell_embed, base):
    rows, width = queries.shape
    sources = [cell_types[None, :], promoters[None, :], offsets[None, :], queries, cell_embed]
    return pl.pallas_call(
        query_kernel,
        in_specs=[SMEM] + [HBM] * 5,
        out_specs=VMEM,
        out_shape=jax.ShapeDtypeStruct((width + EXTRA, rows), jnp.bfloat16),
        scratch_shapes=[pltpu.VMEM(a.shape, a.dtype) for a in sources] + [pltpu.SemaphoreType.DMA((5,))],
        compiler_params=pltpu.CompilerParams(vmem_limit_bytes=QUERY_VMEM),
        name="prepare_queries",
    )(base[None], *sources)


def prepare_bins(values, groups):
    bins = values.shape[0]
    return pl.pallas_call(
        bins_kernel,
        in_specs=[VMEM],
        out_specs=VMEM,
        out_shape=jax.ShapeDtypeStruct((groups, HEAD_DIM + EXTRA, bins), jnp.bfloat16),
        compiler_params=pltpu.CompilerParams(vmem_limit_bytes=16 * 2**20),
        cost_estimate=pl.CostEstimate(flops=0, bytes_accessed=4 * 2**20, transcendentals=0),
        name="prepare_bins",
    )(values)


def attend_near(shifts, seq_count, slopes, position, queries, keys, values):
    groups, depth, bins = values.shape
    n = len(shifts)
    height, rows = queries[0].shape[-2:]
    return pl.pallas_call(
        functools.partial(near_kernel, shifts, seq_count),
        in_specs=[SMEM, SMEM] + [VMEM] * (len(queries) + 2),
        out_specs=VMEM,
        out_shape=jax.ShapeDtypeStruct((n, height, rows), jnp.bfloat16),
        scratch_shapes=[pltpu.VMEM((depth, n * rows), jnp.float32)],
        compiler_params=pltpu.CompilerParams(vmem_limit_bytes=24 * 2**20),
        cost_estimate=pl.CostEstimate(
            flops=4 * n * rows * bins * groups * LANES, bytes_accessed=4 * 2**20, transcendentals=n * rows * bins * groups
        ),
        name="attend_near",
    )(slopes, position[None], *queries, keys, values)


def merge_other(parts, groups):
    return pl.pallas_call(
        functools.partial(other_kernel, groups),
        in_specs=[VMEM] * len(parts),
        out_specs=VMEM,
        out_shape=jax.ShapeDtypeStruct(parts[0].shape[1:], jnp.bfloat16),
        compiler_params=pltpu.CompilerParams(vmem_limit_bytes=8 * 2**20),
        name="merge_other",
    )(*parts)


def merge(place, theirs, parts, w_out, groups):
    rows = theirs.shape[1]
    width = w_out.shape[1] // 4
    return pl.pallas_call(
        functools.partial(merge_kernel, groups),
        in_specs=[SMEM] + [VMEM] * (len(parts) + 2),
        out_specs=[VMEM] * 2,
        out_shape=[
            jax.ShapeDtypeStruct((2, rows, width), jnp.float32),
            jax.ShapeDtypeStruct((2, rows, width), jnp.bfloat16),
        ],
        compiler_params=pltpu.CompilerParams(vmem_limit_bytes=12 * 2**20),
        name="merge",
    )(place[None], theirs, *parts, w_out)


def rotated(value, steps):
    count = lax.axis_size("seq")
    return lax.ppermute(value, "seq", [(i, (i + steps) % count) for i in range(count)])


def swapped(value, axis, bit):
    return lax.ppermute(value, axis, [(i, i ^ bit) for i in range(lax.axis_size(axis))])


def local(queries, cell_types, promoters, offsets, cell_embed, bin_keys, bin_values, slopes, w_out):
    seq_count = lax.axis_size("seq")
    position = lax.axis_index("seq")
    place = lax.axis_index("head")
    bins = bin_keys.shape[0]
    groups = slopes.shape[0]

    mine = prepare_queries(queries, cell_types, promoters, offsets, cell_embed, position * bins)
    other = swapped(mine, "seq", 1)
    values = prepare_bins(bin_values, groups)
    other, values = lax.optimization_barrier((other, values))
    both = jnp.stack([mine, other])
    shifts = [2, -2, 1, -1]
    arrived = [rotated(both, 2 * shift) for shift in shifts]
    part = attend_near(((0, True), (0, False)), seq_count, slopes, position, [mine, other], bin_keys, values)
    parts = [part]
    for k in ORDER:
        shift = shifts[k]
        query = arrived[k]
        if k == ORDER[0]:
            query, _ = lax.optimization_barrier((query, part))
        share = attend_near(((shift, True), (shift, False)), seq_count, slopes, position, [query], bin_keys, values)
        parts.append(rotated(share, -2 * shift))
    theirs = swapped(merge_other(parts, groups), "seq", 1)
    keep, send = merge(place, theirs, parts, w_out, groups)
    got = swapped(send, "head", 1)
    rest = (keep[1] + got[1].astype(jnp.float32)).astype(jnp.bfloat16)
    last = swapped(rest, "head", 2)
    return (keep[0] + got[0].astype(jnp.float32) + last.astype(jnp.float32)).astype(jnp.bfloat16)


def solution(mesh):
    return jax.shard_map(
        local,
        mesh=mesh,
        in_specs=(
            P("seq", "head"),
            P("seq"),
            P("seq"),
            P("seq"),
            P(None, "head"),
            P("seq", "head"),
            P("seq", "head"),
            P("head"),
            P("head", None),
        ),
        out_specs=P("seq", "head"),
        check_vma=False,
    )
```

```python
import functools
import math

import jax
import jax.numpy as jnp
from jax import lax
from jax.experimental import pallas as pl
from jax.experimental.pallas import tpu as pltpu
from jax.sharding import PartitionSpec as P

HEAD_DIM = 96
RADIUS = 7812
SHIFT = 64
LANES = 128
LOG2E = math.log2(math.e)
SCALE2 = LOG2E / math.sqrt(HEAD_DIM)
FAR = 1e30
EMPTY = -16384.0
SUM_LO, SUM_HI = 2.0**-60, 2.0**100
TILE = 512
QUERY_VMEM = 60 * 2**20
EXTRA = 16

SMEM = pl.BlockSpec(memory_space=pltpu.SMEM)
VMEM = pl.BlockSpec(memory_space=pltpu.VMEM)
HBM = pl.BlockSpec(memory_space=pltpu.HBM)


def query_kernel(base_ref, *refs):
    sources, out_ref, copies, sems = refs[:5], refs[5], refs[6:11], refs[11]
    moves = [pltpu.make_async_copy(a, b, sems.at[i]) for i, (a, b) in enumerate(zip(sources, copies))]
    for move in moves:
        move.start()
    for move in moves:
        move.wait()
    types_ref, promoters_ref, offsets_ref, queries_ref, embed_ref = copies
    rows, width = queries_ref.shape
    kinds = embed_ref.shape[0]
    one_hot = (lax.broadcasted_iota(jnp.int32, (kinds, rows), 0) == types_ref[...]).astype(jnp.float32)
    embedded = jnp.dot(one_hot.T.astype(jnp.bfloat16), embed_ref[...], preferred_element_type=jnp.float32)
    query = queries_ref[...].astype(jnp.float32) + embedded
    out_ref[:width, :] = query.T.astype(jnp.bfloat16)
    place = promoters_ref[...] + offsets_ref[...] - base_ref[0] + SHIFT
    coarse = lax.shift_right_arithmetic(place, 4) * 16
    line = lax.broadcasted_iota(jnp.int32, (EXTRA, rows), 0)
    extra = jnp.where(line == 0, coarse, jnp.where(line == 1, place - coarse, 0))
    out_ref[width:, :] = extra.astype(jnp.float32).astype(jnp.bfloat16)


def bins_kernel(values_ref, out_ref):
    groups, _, bins = out_ref.shape
    values = values_ref[...].T
    for g in range(groups):
        out_ref[g, :HEAD_DIM, :] = values[g * HEAD_DIM : (g + 1) * HEAD_DIM]
        out_ref[g, HEAD_DIM:, :] = jnp.ones((EXTRA, bins), jnp.bfloat16)


def block_facts(extra, strides, stride, bins, ok):
    extra = extra.astype(jnp.float32)
    centre = extra[0:1] + extra[1:2] - (stride * bins + SHIFT).astype(jnp.float32)
    before, after = -centre, centre - float(bins - 1)
    if strides == (0,):
        base = jnp.zeros_like(centre)
    elif min(strides) > 0:
        base = before
    elif max(strides) < 0:
        base = after
    else:
        base = jnp.maximum(before, after)
    alive = jnp.where(jnp.maximum(before, after) <= RADIUS, 1.0, 0.0) * jnp.where(ok, 1.0, 0.0)
    return centre, base, alive


def tile_needs(strides, bins, start, size):
    bends, ends = min(strides) <= 0 <= max(strides), False
    for stride in strides:
        low, high = -SHIFT - stride * bins, bins - 1 + SHIFT - stride * bins
        if max(-high, low - (bins - 1)) > RADIUS:
            continue
        if stride >= 0:
            bends |= high > start
            ends |= start + size - 1 - low > RADIUS
        if stride <= 0:
            bends |= low < start + size - 1
            ends |= high - start > RADIUS
    return bends, ends


def attend_rows(blocks, strides, oks, slopes, query_refs, keys_ref, values_ref, out_refs, acc_ref):
    bins, width = keys_ref.shape
    groups = values_ref.shape[0]
    rows = query_refs[0].shape[1]
    n = len(query_refs)
    parts = [slice(i * rows, (i + 1) * rows) for i in range(n)]
    facts = [block_facts(ref[width:, :], *each, bins, ok) for ref, *each, ok in zip(query_refs, blocks, strides, oks)]
    centre, base, alive = (jnp.concatenate([fact[k] for fact in facts], axis=1) for k in range(3))
    alive = alive > 0.0
    windows, queries = [], []
    for g in range(groups):
        low, high = g * HEAD_DIM, (g + 1) * HEAD_DIM
        first, last = low // LANES * LANES, -(-high // LANES) * LANES
        query = jnp.concatenate([ref[low:high, :] for ref in query_refs], axis=1)
        pads = [jnp.zeros((size, n * rows), jnp.bfloat16) for size in (low - first, last - high)]
        pieces = [piece for piece in (pads[0], query, pads[1]) if piece.shape[0]]
        windows.append(slice(first, last))
        queries.append(jnp.concatenate(pieces, axis=0))

    def products(g, start, size):
        return jnp.dot(keys_ref[pl.ds(start, size), windows[g]], queries[g], preferred_element_type=jnp.float32)

    def positions(start, size):
        return (start + lax.broadcasted_iota(jnp.int32, (size, 1), 0)).astype(jnp.float32)

    line = lax.broadcasted_iota(jnp.int32, (EXTRA, n * rows), 0)

    def finish(g, acc, shift, extra):
        exponent = shift - slopes[g] * base
        coarse = jnp.where(alive, jnp.round(exponent * 0.0625) * 16.0, EMPTY)
        factor = jnp.where(alive, jnp.exp2(exponent - coarse), 0.0)
        scaled = jnp.where(alive, acc * factor, 0.0)
        total = scaled[HEAD_DIM : HEAD_DIM + 1]
        high = total.astype(jnp.bfloat16).astype(jnp.float32)
        for part, ref in zip(parts, out_refs):
            ref[g * HEAD_DIM : (g + 1) * HEAD_DIM, :] = scaled[:HEAD_DIM, part].astype(jnp.bfloat16)
        for k, row in enumerate((high, total - high, coarse)):
            extra = jnp.where(line == k * groups + g, row, extra)
        return extra

    def finished(extra):
        for part, ref in zip(parts, out_refs):
            ref[width:, :] = extra[:, part].astype(jnp.bfloat16)

    accs = [None] * groups
    for start in range(0, bins, TILE):
        position = positions(start, TILE)
        shapes = []
        for block, (middle, origin, _) in zip(blocks, facts):
            bends, ends = tile_needs(block, bins, start, TILE)
            if bends:
                distance = jnp.abs(position - middle) - origin
            else:
                distance = position if min(block) > 0 else float(bins - 1) - position
            shapes.append((distance, jnp.abs(position - middle) <= RADIUS if ends else None))
        weights = []
        for g in range(groups):
            raw = products(g, start, TILE)
            pieces = []
            for part, (distance, usable) in zip(parts, shapes):
                weight = jnp.exp2(raw[:, part] * SCALE2 - slopes[g] * distance)
                weight = weight if usable is None else jnp.where(usable, weight, 0.0)
                pieces.append(weight.astype(jnp.bfloat16))
            weights.append(jnp.concatenate(pieces, axis=1))
        for g in range(groups):
            gained = jnp.dot(values_ref[g, :, start : start + TILE], weights[g], preferred_element_type=jnp.float32)
            accs[g] = gained if accs[g] is None else accs[g] + gained
    wrong = jnp.zeros((1, n * rows), jnp.float32)
    extra = jnp.zeros((EXTRA, n * rows), jnp.float32)
    for g in range(groups):
        total = accs[g][HEAD_DIM : HEAD_DIM + 1]
        wrong = jnp.where((total >= SUM_LO) & (total <= SUM_HI), wrong, 1.0)
        extra = finish(g, accs[g], 0.0, extra)
    finished(extra)

    @pl.when(jnp.max(jnp.where(alive, wrong, 0.0)) > 0.0)
    def _():
        extra = jnp.zeros((EXTRA, n * rows), jnp.float32)
        for g in range(groups):

            def logs(k):
                start = pl.multiple_of(k * LANES, LANES)
                distance = jnp.abs(positions(start, LANES) - centre)
                exponent = products(g, start, LANES) * SCALE2 - slopes[g] * (distance - base)
                return start, jnp.where(distance <= RADIUS, exponent, -FAR)

            def largest(k, so_far):
                return jnp.maximum(so_far, jnp.max(logs(k)[1], axis=0, keepdims=True))

            shift = lax.fori_loop(0, bins // LANES, largest, jnp.full((1, n * rows), -FAR, jnp.float32))
            acc_ref[...] = jnp.zeros_like(acc_ref)

            @pl.loop(0, bins // LANES)
            def _(k):
                start, exponent = logs(k)
                weights = jnp.exp2(exponent - shift).astype(jnp.bfloat16)
                acc_ref[...] += jnp.dot(values_ref[g, :, pl.ds(start, LANES)], weights, preferred_element_type=jnp.float32)

            extra = finish(g, acc_ref[...], shift, extra)
        finished(extra)


def near_kernel(shifts, seq_count, slopes_ref, position_ref, *refs):
    query_refs, (keys_ref, values_ref, out_ref, acc_ref) = refs[:-4], refs[-4:]
    if len(query_refs[0].shape) == 3:
        query_refs = [query_refs[0].at[i] for i in range(len(shifts))]
    position = position_ref[0]
    odd = position & 1
    blocks, strides, oks = [], [], []
    for even_stride, odd_stride in shifts:
        stride = even_stride + (odd_stride - even_stride) * odd
        blocks.append(tuple(sorted({even_stride, odd_stride})))
        strides.append(stride)
        oks.append((position - stride >= 0) & (position - stride < seq_count))
    attend_rows(
        blocks,
        strides,
        oks,
        [slopes_ref[g] * LOG2E for g in range(values_ref.shape[0])],
        query_refs,
        keys_ref,
        values_ref,
        [out_ref.at[i] for i in range(len(shifts))],
        acc_ref,
    )


def combined(groups, refs):
    width = groups * HEAD_DIM
    extras = [ref[width:, :].astype(jnp.float32) for ref in refs]
    found = []
    for g in range(groups):
        scales = [extra[2 * groups + g : 2 * groups + g + 1] for extra in extras]
        top = functools.reduce(jnp.maximum, scales)
        acc, total = 0.0, 0.0
        for ref, extra, scale in zip(refs, extras, scales):
            factor = jnp.exp2(scale - top)
            acc += ref[g * HEAD_DIM : (g + 1) * HEAD_DIM, :].astype(jnp.float32) * factor
            total += (extra[g : g + 1] + extra[groups + g : groups + g + 1]) * factor
        found.append((acc, total, top))
    return found


def other_kernel(groups, *refs):
    part_refs, out_ref = refs[:-1], refs[-1]
    width = groups * HEAD_DIM
    line = lax.broadcasted_iota(jnp.int32, (EXTRA, out_ref.shape[1]), 0)
    extra = jnp.zeros(line.shape, jnp.float32)
    for g, (acc, total, top) in enumerate(combined(groups, [ref.at[1] for ref in part_refs])):
        high = total.astype(jnp.bfloat16).astype(jnp.float32)
        for k, row in enumerate((high, total - high, top)):
            extra = jnp.where(line == k * groups + g, row, extra)
        out_ref[g * HEAD_DIM : (g + 1) * HEAD_DIM, :] = acc.astype(jnp.bfloat16)
    out_ref[width:, :] = extra.astype(jnp.bfloat16)


def merge_kernel(groups, place_ref, theirs_ref, *refs):
    part_refs, (w_ref, keep_ref, send_ref) = refs[:-3], refs[-3:]
    shares = combined(groups, [theirs_ref] + [ref.at[0] for ref in part_refs])
    pooled = jnp.concatenate([acc / total for acc, total, _ in shares], axis=0).T.astype(jnp.bfloat16)
    width = w_ref.shape[1] // 4
    core, high = place_ref[0] & 1, place_ref[0] >> 1
    for k in range(2):
        row = (high if k == 0 else 1 - high) * 2
        for ref, lane in ((send_ref, 1 - core), (keep_ref, core)):
            start = pl.multiple_of((row + lane) * width, LANES)
            ref[k] = jnp.dot(pooled, w_ref[:, pl.ds(start, width)], preferred_element_type=jnp.float32).astype(ref.dtype)


def prepare_queries(queries, cell_types, promoters, offsets, cell_embed, base):
    rows, width = queries.shape
    sources = [cell_types[None, :], promoters[None, :], offsets[None, :], queries, cell_embed]
    return pl.pallas_call(
        query_kernel,
        in_specs=[SMEM] + [HBM] * 5,
        out_specs=VMEM,
        out_shape=jax.ShapeDtypeStruct((width + EXTRA, rows), jnp.bfloat16),
        scratch_shapes=[pltpu.VMEM(a.shape, a.dtype) for a in sources] + [pltpu.SemaphoreType.DMA((5,))],
        compiler_params=pltpu.CompilerParams(vmem_limit_bytes=QUERY_VMEM),
        name="prepare_queries",
    )(base[None], *sources)


def prepare_bins(values, groups):
    bins = values.shape[0]
    return pl.pallas_call(
        bins_kernel,
        in_specs=[VMEM],
        out_specs=VMEM,
        out_shape=jax.ShapeDtypeStruct((groups, HEAD_DIM + EXTRA, bins), jnp.bfloat16),
        compiler_params=pltpu.CompilerParams(vmem_limit_bytes=16 * 2**20),
        cost_estimate=pl.CostEstimate(flops=0, bytes_accessed=4 * 2**20, transcendentals=0),
        name="prepare_bins",
    )(values)


def attend_near(shifts, seq_count, slopes, position, queries, keys, values):
    groups, depth, bins = values.shape
    n = len(shifts)
    height, rows = queries[0].shape[-2:]
    return pl.pallas_call(
        functools.partial(near_kernel, shifts, seq_count),
        in_specs=[SMEM, SMEM] + [VMEM] * (len(queries) + 2),
        out_specs=VMEM,
        out_shape=jax.ShapeDtypeStruct((n, height, rows), jnp.bfloat16),
        scratch_shapes=[pltpu.VMEM((depth, n * rows), jnp.float32)],
        compiler_params=pltpu.CompilerParams(vmem_limit_bytes=24 * 2**20),
        cost_estimate=pl.CostEstimate(
            flops=4 * n * rows * bins * groups * LANES, bytes_accessed=4 * 2**20, transcendentals=n * rows * bins * groups
        ),
        name="attend_near",
    )(slopes, position[None], *queries, keys, values)


def merge_other(parts, groups):
    return pl.pallas_call(
        functools.partial(other_kernel, groups),
        in_specs=[VMEM] * len(parts),
        out_specs=VMEM,
        out_shape=jax.ShapeDtypeStruct(parts[0].shape[1:], jnp.bfloat16),
        compiler_params=pltpu.CompilerParams(vmem_limit_bytes=8 * 2**20),
        name="merge_other",
    )(*parts)


def merge(place, theirs, parts, w_out, groups):
    rows = theirs.shape[1]
    width = w_out.shape[1] // 4
    return pl.pallas_call(
        functools.partial(merge_kernel, groups),
        in_specs=[SMEM] + [VMEM] * (len(parts) + 2),
        out_specs=[VMEM] * 2,
        out_shape=[
            jax.ShapeDtypeStruct((2, rows, width), jnp.float32),
            jax.ShapeDtypeStruct((2, rows, width), jnp.bfloat16),
        ],
        compiler_params=pltpu.CompilerParams(vmem_limit_bytes=12 * 2**20),
        name="merge",
    )(place[None], theirs, *parts, w_out)


def rotated(value, steps, mirrored=False):
    count = lax.axis_size("seq")
    moves = [-steps if mirrored and i % 2 else steps for i in range(count)]
    return lax.ppermute(value, "seq", [(i, (i + move) % count) for i, move in enumerate(moves)])


def swapped(value, axis, bit):
    return lax.ppermute(value, axis, [(i, i ^ bit) for i in range(lax.axis_size(axis))])


def local(queries, cell_types, promoters, offsets, cell_embed, bin_keys, bin_values, slopes, w_out):
    seq_count = lax.axis_size("seq")
    position = lax.axis_index("seq")
    place = lax.axis_index("head")
    bins = bin_keys.shape[0]
    groups = slopes.shape[0]

    mine = prepare_queries(queries, cell_types, promoters, offsets, cell_embed, position * bins)
    other = swapped(mine, "seq", 1)
    values = prepare_bins(bin_values, groups)
    other, values = lax.optimization_barrier((other, values))
    both = jnp.stack([mine, other])
    outward = [rotated(both, 4, True), rotated(mine, -4, True), rotated(both, 2), rotated(both, -2)]
    reach = [((4, -4), (3, -3)), ((-4, 4),), ((2, 2), (1, 3)), ((-2, -2), (-3, -1))]
    back = [(-4, True), (4, True), (-2, False), (2, False)]
    home = attend_near(((0, 0), (-1, 1)), seq_count, slopes, position, [mine, other], bin_keys, values)
    shares = [attend_near(blocks, seq_count, slopes, position, [query], bin_keys, values) for query, blocks in zip(outward, reach)]
    far, farther, up, down = [rotated(share, *steps) for share, steps in zip(shares, back)]
    parts = [home, up, down, far]
    theirs = swapped(merge_other(parts, groups), "seq", 1)
    keep, send = merge(place, theirs, parts + [farther], w_out, groups)
    got = swapped(send, "head", 1)
    rest = (keep[1] + got[1].astype(jnp.float32)).astype(jnp.bfloat16)
    last = swapped(rest, "head", 2)
    return (keep[0] + got[0].astype(jnp.float32) + last.astype(jnp.float32)).astype(jnp.bfloat16)


def solution(mesh):
    return jax.shard_map(
        local,
        mesh=mesh,
        in_specs=(
            P("seq", "head"),
            P("seq"),
            P("seq"),
            P("seq"),
            P(None, "head"),
            P("seq", "head"),
            P("seq", "head"),
            P("head"),
            P("head", None),
        ),
        out_specs=P("seq", "head"),
        check_vma=False,
    )
```
